128 devices in a mesh: blk: 16 (over z, y_lo, core), aux: 8 (over y_hi, x).
Axes of the slice: x: 4, y: 4 (y_hi: 2, y_lo: 2; y = y_hi * 2 + y_lo), z: 4, core: 2. Of those that a mesh axis runs over, the one named last changes fastest.
Arguments:
- coeffs: float32 [2048, 256], P('blk'), may hold values from -6 to 6
- integrals: float32 [16, 128, 128, 16, 128], P('blk', 'aux'), may hold values from -0.01953125 to 0.01953125
- metric: float32 [128, 128], replicated, as said below
- pair_blocks: int32 [16, 16], P('blk'), may hold values from 0 to 15, as said below
- support: int32 [256, 4], replicated, may hold values from 0 to 15, as said below
Outputs:
- exchange_band: float32 [2048, 128], P(('blk', 'aux'))
The draws below stay inside these ranges and needn't reach their ends.
Inputs may be any that keep to these rules, and one draw needn't show every extreme that they name: `pair_blocks`: each row lists 16 distinct blocks, and row r lists block r first. `support`: each orbital lists 4 distinct blocks. `metric`: symmetric.
All inputs are finite; a program needn't handle non-finite values.
Results may differ from the reference program's by a relative error of at most 0.000061.
Values sent between devices are 32-bit elements; how exact they have to be, the bound alone decides.
A program may use at most 128 MiB of HBM per device.

```python
import jax
import jax.numpy as jnp
from jax import lax

S = 128
BLOCKS_DEV = 1
PAIRS = 16
NAUX = 128
NOCC = 256
NBLK = 16
NBAS = 2048
BAND = 128
SUPP = 4


def distinct_picks(key, rows, first, count):
    raw = jax.random.randint(key, (rows, NBLK), 0, 4096)
    scores = raw * NBLK + jnp.arange(NBLK, dtype=jnp.int32)[None, :]
    forced = jnp.arange(NBLK, dtype=jnp.int32)[None, :] == first[:, None]
    scores = jnp.where(forced, 4096 * NBLK + NBLK, scores)
    values, picked = lax.top_k(scores, count)
    return picked.astype(jnp.int32)


def draw_pair_blocks(key, part):
    key = jax.random.fold_in(key, 11)
    return distinct_picks(key, NBLK, jnp.arange(NBLK, dtype=jnp.int32), PAIRS)


def draw_support(key, part):
    key = jax.random.fold_in(key, 23)
    homes = jnp.arange(NOCC, dtype=jnp.int32) * NBLK // NOCC
    return distinct_picks(key, NOCC, homes, SUPP)


def draw_metric(key, part):
    key = jax.random.fold_in(key, 37)
    noise = jax.random.normal(key, (NAUX, NAUX), jnp.float32)
    return jnp.eye(NAUX, dtype=jnp.float32) + (noise + noise.T) * (0.35 * NAUX ** (-0.5))


def steps_of(own_key, extent, cuts, smallest, high):
    factor_of = 1.0
    for axis_at, shards_of in cuts:
        heights = jax.random.uniform(jax.random.fold_in(jax.random.fold_in(own_key, 6), axis_at), (shards_of,), jnp.float32, smallest / len(cuts), high / len(cuts))
        factor_of = factor_of * jnp.repeat(jnp.exp(heights), extent[axis_at] // shards_of).reshape((-1,) + (1,) * (len(extent) - 1 - axis_at))
    return factor_of


def normal_values(own_key, shape, spread, reach, cuts=(), kind=jnp.bfloat16):
    values = jax.random.normal(own_key, shape, jnp.float32) * spread
    if len(cuts) > 0:
        values = steps_of(own_key, shape, cuts, -0.22, 0.18) * values
    return jnp.clip(values, min=-reach, max=reach).astype(kind)


def setup_inputs(seed: int = 0) -> dict:
    seeds = jax.random.split(jax.random.key(seed), 6)
    coeffs = normal_values(seeds[0], (NBAS, NOCC), 1.0, 6.0, ((0, 16),), jnp.float32)
    integrals = normal_values(seeds[1], (NBLK, NAUX, S, PAIRS, S), (PAIRS * S * 54) ** -0.5, 0.01953125, ((0, 16), (1, 8)), jnp.float32)
    metric = draw_metric(jax.random.fold_in(seeds[5], 71), 0)
    pair_blocks = draw_pair_blocks(jax.random.fold_in(seeds[5], 71), 0)
    support = draw_support(jax.random.fold_in(seeds[5], 71), 0)
    return dict(coeffs=coeffs, integrals=integrals, metric=metric, pair_blocks=pair_blocks, support=support)


def reference(coeffs, integrals, metric, pair_blocks, support):
    hi = lax.Precision.HIGHEST
    blocks = jnp.arange(NBLK, dtype=jnp.int32)
    hit = jnp.any(support[:, :, None] == blocks[None, None, :], axis=1)
    masked = coeffs.reshape(NBLK, S, NOCC) * jnp.transpose(hit).astype(jnp.float32)[:, None, :]
    groups = NBLK // BLOCKS_DEV
    ints_g = integrals.reshape(groups, BLOCKS_DEV, NAUX * S, PAIRS * S)
    pairs_g = pair_blocks.reshape(groups, BLOCKS_DEV, PAIRS)

    def one_group(item):
        ints, pairs = item
        paired = masked[pairs].reshape(BLOCKS_DEV, PAIRS * S, NOCC)
        half = jnp.einsum("bxk,bki->bxi", ints, paired, precision=hi).reshape(BLOCKS_DEV, NAUX, S, NOCC)
        fitted = jnp.einsum("pq,bqmi->bpmi", metric, half, precision=hi)
        band = jnp.einsum("bpmi,cpni->bmcn", half, fitted, precision=hi)
        return band.reshape(BLOCKS_DEV * S, BLOCKS_DEV * S)

    bands = lax.map(one_group, (ints_g, pairs_g))
    return bands.reshape(NBAS, BAND)
```

```python
import functools

import jax
import jax.numpy as jnp
from jax import lax
from jax.experimental import pallas as pl
from jax.experimental.pallas import tpu as pltpu
from jax.sharding import PartitionSpec as P

S = 128
PAIRS = 16
NOCC = 256
SHARE = 16
NAUX = 128
K = PAIRS * S
QROWS = 64
CHUNKS = ((0, 64), (64, 64), (128, 128))
NGROUPS = 8
f32, bf16 = jnp.float32, jnp.bfloat16
MESH = pl.DeviceIdType.MESH
NN = (((1,), (0,)), ((), ()))
NT = (((1,), (1,)), ((), ()))
PEERS = [(dx, dy) for dy in (1, 0) for dx in (2, 1, 3, 0) if (dx, dy) != (0, 0)]
GATHER = [(1, 2), (1, 1), (1, 3), (0, 2), (0, 1), (0, 3), (1, 0)]


def split(v):
    hi = v.astype(bf16)
    return hi, (v - hi.astype(f32)).astype(bf16)


def dot3(a, b, dims=NN):
    ah, al = a
    bh, bl = b
    d = functools.partial(lax.dot_general, dimension_numbers=dims, preferred_element_type=f32)
    return d(ah, bh) + (d(ah, bl) + d(al, bh))


def kernel(
    pair_ref, coeffs_hbm, support_hbm, metric_hbm, ints_ref, out_ref,
    coeffs_ref, support_ref, metric_ref, ints, i_hi, i_lo, ct0, ct1, ct2, lhs0, lhs1, lhs01, lhs2, half01, half23, recv01, recv23, band, bands,
    in_sem, i_sem, g_send, g_recv, y_send, y_recv, z_send, z_recv, c_send, c_recv, a_send, a_recv, b_send, b_recv,
):
    blk, aux = lax.axis_index("blk"), lax.axis_index("aux")
    core, ylo, z = lax.rem(blk, 2), lax.rem(blk // 2, 2), blk // 4
    x, yhi = lax.rem(aux, 4), aux // 4
    y = yhi * 2 + ylo
    zy = z * 2 + ylo
    cts = (ct0, ct1, ct2)

    def device(x, y, z, core):
        return ((z * 2 + lax.rem(y, 2)) * 2 + core, (y // 2) * 4 + x)

    def aux_peer(dx, dy):
        return lax.rem(yhi + dy, 2) * 4 + lax.rem(x + dx, 4)

    def gather_peer(oy, dz, sign):
        step = oy * (1 + 2 * core) if sign > 0 else oy * (3 - 2 * core)
        return device(x, lax.rem(y + step, 4), lax.rem(z + (dz if sign > 0 else 4 - dz), 4), core)

    sibling = (blk + 1 - 2 * core, aux)

    inputs = []
    for i, (src, dst) in enumerate(
        ((coeffs_hbm, coeffs_ref), (support_hbm, support_ref), (metric_hbm, metric_ref))
    ):
        load = pltpu.make_async_copy(src, dst, in_sem.at[i])
        load.start()
        inputs.append(load)
    barrier = pltpu.get_barrier_semaphore()
    for oy, dz in GATHER:
        pl.semaphore_signal(barrier, inc=1, device_id=gather_peer(oy, dz, -1), device_id_type=MESH)
    for dx, dy in PEERS:
        pl.semaphore_signal(barrier, inc=1, device_id=(blk, aux_peer(dx, dy)), device_id_type=MESH)
    pl.semaphore_signal(barrier, inc=1, device_id=sibling, device_id_type=MESH)

    inputs[0].wait()
    inputs[1].wait()
    loads = []
    rows = SHARE * S * PAIRS // NGROUPS
    for g in range(NGROUPS):
        load = pltpu.make_async_copy(
            ints_ref.at[pl.ds(g * rows, rows)], ints.at[pl.ds(g * rows, rows)], i_sem.at[g]
        )
        load.start()
        loads.append(load)

    hit = jnp.max((support_ref[...] == blk).astype(f32), axis=0, keepdims=True)
    masked = (coeffs_ref[...] * hit).T
    for ct, (first, n) in zip(cts, CHUNKS):
        ct[core, zy] = masked[first:first + n]

    pl.semaphore_wait(barrier, len(GATHER) + len(PEERS) + 1)

    sends, y_sends, z_sends = [], [None], [None]

    def across_y(k):
        copy = pltpu.make_async_remote_copy(
            src_ref=cts[k].at[core, zy], dst_ref=cts[k].at[core, zy],
            send_sem=y_send.at[k - 1], recv_sem=y_recv.at[k - 1],
            device_id=gather_peer(1, 0, 1), device_id_type=MESH,
        )
        copy.start()
        y_sends.append(copy)

    across_y(1)
    for i, (oy, dz) in enumerate(GATHER):
        copy = pltpu.make_async_remote_copy(
            src_ref=ct0.at[core, zy], dst_ref=ct0.at[core, zy],
            send_sem=g_send.at[i], recv_sem=g_recv.at[i],
            device_id=gather_peer(oy, dz, 1), device_id_type=MESH,
        )
        copy.start()
        sends.append(copy)
    across_y(2)

    def along_z(k):
        y_sends[k].wait_recv()
        both = cts[k].at[core, pl.ds(z * 2, 2)]
        z_sends.append([])
        for i, dz in enumerate((2, 1, 3)):
            copy = pltpu.make_async_remote_copy(
                src_ref=both, dst_ref=both,
                send_sem=z_send.at[k - 1, i], recv_sem=z_recv.at[k - 1, i],
                device_id=gather_peer(0, dz, 1), device_id_type=MESH,
            )
            copy.start()
            z_sends[k].append(copy)

    def split_ints(g):
        loads[g].wait()

        def part(t, carry):
            at = pl.multiple_of(g * 256 + t * 64, 64)
            for p in range(PAIRS):
                hi, lo = split(ints[pl.ds(at * PAIRS + p, 64, stride=PAIRS), :])
                i_hi[pl.ds(at, 64), p * S:(p + 1) * S] = hi
                i_lo[pl.ds(at, 64), p * S:(p + 1) * S] = lo
            return carry

        lax.fori_loop(0, 4, part, 0)

    def forward(k):
        for copy in sends if k == 0 else z_sends[k]:
            copy.wait_recv()
        copy = pltpu.make_async_remote_copy(
            src_ref=cts[k].at[core], dst_ref=cts[k].at[core],
            send_sem=c_send.at[k], recv_sem=c_recv.at[k],
            device_id=sibling, device_id_type=MESH,
        )
        copy.start()
        return copy

    def assemble(k, copy, *places):
        copy.wait_recv()
        ct, n = cts[k], CHUNKS[k][1]
        for p in range(PAIRS):
            b = pair_ref[0, p]
            parts = split(ct[lax.rem(b, 2), b // 2])
            for lhs, *firsts in places:
                for first, part in zip(firsts, parts):
                    lhs[first:first + n, p * S:(p + 1) * S] = part

    def send(k, source, target, at, count):
        for dx, dy in PEERS:
            a = aux_peer(dx, dy)
            pltpu.make_async_remote_copy(
                src_ref=source(a, pl.ds(at, count)), dst_ref=target(pl.ds(aux * SHARE + at, count)),
                send_sem=a_send.at[k], recv_sem=a_recv.at[k],
                device_id=(blk, a), device_id_type=MESH,
            ).start()
        pltpu.make_async_copy(
            source(aux, pl.ds(at, count)), target(pl.ds(aux * SHARE + at, count)), a_recv.at[k]
        ).start()

    def send01(first, rows):
        o = pl.ds(first, rows)
        return functools.partial(
            send, 0, lambda a, at: half01.at[a, at, o], lambda at: recv01.at[at, o]
        )

    def send23(i):
        return functools.partial(
            send, 1 + i, lambda a, at: half23.at[i, a, at], lambda at: recv23.at[i, at]
        )

    def products(lhs, q, low, high, step):
        n = lhs.shape[0] // 2
        quarters = [q + r for r in range(n // QROWS)]

        def group(g, carry):
            at = pl.ds(pl.multiple_of(g * step * S, step * S), step * S)
            both = jnp.zeros((2 * n, step * S), f32)
            cross = jnp.zeros((n, step * S), f32)
            for j in range(K // 256):
                c = slice(j * 256, (j + 1) * 256)
                both += lax.dot_general(lhs[:, c], i_hi[at, c], NT, preferred_element_type=f32)
                cross += lax.dot_general(lhs[0:n, c], i_lo[at, c], NT, preferred_element_type=f32)
            total = both[:n] + (both[n:] + cross)
            for j in range(step):
                for i, r in enumerate(quarters):
                    rows = total[i * QROWS:(i + 1) * QROWS, j * S:(j + 1) * S].reshape(8, 8, S)
                    if r < 2:
                        half01[:, g * step + j, r * 8:r * 8 + 8] = rows
                    else:
                        half23[r - 2, :, g * step + j] = rows
            if q < 2:
                send01(q * 8, 8 * len(quarters))(g * step, step)
            else:
                send23(0)(g * step, step)
            return carry

        lax.fori_loop(low // step, high // step, group, 0)

    inputs[2].wait()
    metric = split(metric_ref[...])

    def arrived(k, buffer):
        pltpu.make_async_copy(buffer, buffer, a_recv.at[k]).wait()

    def finish(buffer, first):
        n = buffer.shape[1]
        flat = buffer.reshape(NAUX * n, S)
        parts = [flat[pl.ds(first + t, NAUX, stride=n), :] for t in range(8)]
        fitted = dot3(metric, split(jnp.concatenate(parts, axis=1)))
        fitted = jnp.concatenate([fitted[:, t * S:(t + 1) * S] for t in range(8)], axis=0)
        turned = jnp.concatenate([v.T for v in parts], axis=1)
        return dot3(split(turned), split(fitted))

    for g in range(4):
        split_ints(g)
    along_z(1)
    split_ints(4)
    f0 = forward(0)
    for g in range(5, NGROUPS):
        split_ints(g)
    along_z(2)
    assemble(0, f0, (lhs0, 0, QROWS), (lhs01, 0, 2 * QROWS))
    products(lhs0, 0, 0, 4, 2)
    f1 = forward(1)
    products(lhs0, 0, 4, 8, 4)
    assemble(1, f1, (lhs1, 0, QROWS), (lhs01, QROWS, 3 * QROWS))
    products(lhs01, 0, 8, SHARE, 2)
    products(lhs1, 1, 0, 4, 4)
    f2 = forward(2)
    products(lhs1, 1, 4, 8, 4)
    assemble(2, f2, (lhs2, 0, 2 * QROWS))
    products(lhs2, 2, 0, 8, 4)
    send23(1)(0, 8)
    products(lhs2, 2, 8, SHARE, 4)
    send23(1)(8, 8)
    arrived(0, recv01)
    band[...] = finish(recv01, 0)
    band[...] += finish(recv01, 8)
    for i in range(2):
        arrived(1 + i, recv23.at[i])
        band[...] += finish(recv23.at[i], 0)

    last = []
    for i, (dx, dy) in enumerate(PEERS):
        a = aux_peer(dx, dy)
        copy = pltpu.make_async_remote_copy(
            src_ref=band.at[pl.ds(pl.multiple_of(a * 16, 16), 16)], dst_ref=bands.at[i],
            send_sem=b_send.at[i], recv_sem=b_recv.at[i],
            device_id=(blk, a), device_id_type=MESH,
        )
        copy.start()
        last.append(copy)
    total = band[pl.ds(pl.multiple_of(aux * 16, 16), 16), :]
    for i, copy in enumerate(last):
        copy.wait_recv()
        total += bands[i]
    out_ref[...] = total

    for copy in sends + y_sends[1:] + z_sends[1] + z_sends[2] + [f0, f1, f2] + last:
        copy.wait_send()
    for k, sent in enumerate((half01.at[pl.ds(0, 7)], half23.at[0, pl.ds(0, 7)], half23.at[1, pl.ds(0, 7)])):
        pltpu.make_async_copy(sent, sent, a_send.at[k]).wait()


def local(coeffs, integrals, metric, pair_blocks, support):
    vmem = pl.BlockSpec(memory_space=pltpu.VMEM)
    dma = pltpu.SemaphoreType.DMA
    return pl.pallas_call(
        kernel,
        name="exchange",
        out_shape=jax.ShapeDtypeStruct((16, S), f32),
        in_specs=[pl.BlockSpec(memory_space=pltpu.SMEM)] + [pl.BlockSpec(memory_space=pl.ANY)] * 4,
        out_specs=vmem,
        scratch_shapes=[
            pltpu.VMEM((S, NOCC), f32),
            pltpu.VMEM((4, NOCC), jnp.int32),
            pltpu.VMEM((S, S), f32),
            pltpu.VMEM((SHARE * S * PAIRS, S), f32),
            pltpu.VMEM((SHARE * S, K), bf16),
            pltpu.VMEM((SHARE * S, K), bf16),
            *[pltpu.VMEM((2, 8, n, S), f32) for _, n in CHUNKS],
            *[pltpu.VMEM((2 * n, K), bf16) for n in (64, 64, 128, 128)],
            pltpu.VMEM((8, SHARE, 16, S), f32),
            pltpu.VMEM((2, 8, SHARE, 8, S), f32),
            pltpu.VMEM((NAUX, 16, S), f32),
            pltpu.VMEM((2, NAUX, 8, S), f32),
            pltpu.VMEM((S, S), f32),
            pltpu.VMEM((len(PEERS), 16, S), f32),
            dma((3,)),
            dma((NGROUPS,)),
            dma((len(GATHER),)),
            dma((len(GATHER),)),
            dma((2,)),
            dma((2,)),
            dma((2, 3)),
            dma((2, 3)),
            dma((3,)),
            dma((3,)),
            dma((3,)),
            dma((3,)),
            dma((len(PEERS),)),
            dma((len(PEERS),)),
        ],
        compiler_params=pltpu.CompilerParams(
            collective_id=0, has_side_effects=True, vmem_limit_bytes=56 * 2**20
        ),
    )(pair_blocks, coeffs, support.T, metric, integrals.reshape(SHARE * S * PAIRS, S))


def solution(mesh):
    return jax.shard_map(
        local,
        mesh=mesh,
        in_specs=(P("blk", None), P("blk", "aux", None, None, None), P(), P("blk", None), P()),
        out_specs=P(("blk", "aux"), None),
        check_vma=False,
    )
```

```python
import functools

import jax
import jax.numpy as jnp
from jax import lax
from jax.experimental import pallas as pl
from jax.experimental.pallas import tpu as pltpu
from jax.sharding import PartitionSpec as P

S = 128
PAIRS = 16
NOCC = 256
SHARE = 16
NAUX = 128
K = PAIRS * S
QROWS = 64
CHUNKS = ((0, 64), (64, 64), (128, 128))
NGROUPS = 8
f32, bf16 = jnp.float32, jnp.bfloat16
MESH = pl.DeviceIdType.MESH
NN = (((1,), (0,)), ((), ()))
NT = (((1,), (1,)), ((), ()))
PEERS = [(dx, dy) for dy in (1, 0) for dx in (2, 1, 3, 0) if (dx, dy) != (0, 0)]
GATHER = [(1, 2), (1, 1), (1, 3), (0, 2), (0, 1), (0, 3), (1, 0)]


def split(v):
    hi = v.astype(bf16)
    return hi, (v - hi.astype(f32)).astype(bf16)


def dot3(a, b, dims=NN):
    ah, al = a
    bh, bl = b
    d = functools.partial(lax.dot_general, dimension_numbers=dims, preferred_element_type=f32)
    return d(ah, bh) + (d(ah, bl) + d(al, bh))


def kernel(
    pair_ref, coeffs_hbm, support_hbm, metric_hbm, ints_ref, out_ref,
    coeffs_ref, support_ref, metric_ref, ints, i_hi, i_lo, ct0, ct1, ct2, lhs0, lhs1, lhs01, lhs2, half01, half23, recv01, recv23, band, bands,
    in_sem, i_sem, g_send, g_recv, y_send, y_recv, z_send, z_recv, c_send, c_recv, a_send, a_recv, b_send, b_recv,
):
    blk, aux = lax.axis_index("blk"), lax.axis_index("aux")
    core, ylo, z = lax.rem(blk, 2), lax.rem(blk // 2, 2), blk // 4
    x, yhi = lax.rem(aux, 4), aux // 4
    y = yhi * 2 + ylo
    zy = z * 2 + ylo
    cts = (ct0, ct1, ct2)

    def device(x, y, z, core):
        return ((z * 2 + lax.rem(y, 2)) * 2 + core, (y // 2) * 4 + x)

    def aux_peer(dx, dy):
        return lax.rem(yhi + dy, 2) * 4 + lax.rem(x + dx, 4)

    def gather_peer(oy, dz, sign):
        step = oy * (1 + 2 * core) if sign > 0 else oy * (3 - 2 * core)
        return device(x, lax.rem(y + step, 4), lax.rem(z + (dz if sign > 0 else 4 - dz), 4), core)

    sibling = (blk + 1 - 2 * core, aux)

    inputs = []
    for i, (src, dst) in enumerate(
        ((coeffs_hbm, coeffs_ref), (support_hbm, support_ref), (metric_hbm, metric_ref))
    ):
        load = pltpu.make_async_copy(src, dst, in_sem.at[i])
        load.start()
        inputs.append(load)
    barrier = pltpu.get_barrier_semaphore()
    for oy, dz in GATHER:
        pl.semaphore_signal(barrier, inc=1, device_id=gather_peer(oy, dz, -1), device_id_type=MESH)
    for dx, dy in PEERS:
        pl.semaphore_signal(barrier, inc=1, device_id=(blk, aux_peer(dx, dy)), device_id_type=MESH)
    pl.semaphore_signal(barrier, inc=1, device_id=sibling, device_id_type=MESH)

    inputs[0].wait()
    inputs[1].wait()
    loads = []
    rows = SHARE * S * PAIRS // NGROUPS
    for g in range(NGROUPS):
        load = pltpu.make_async_copy(
            ints_ref.at[pl.ds(g * rows, rows)], ints.at[pl.ds(g * rows, rows)], i_sem.at[g]
        )
        load.start()
        loads.append(load)

    hit = jnp.max((support_ref[...] == blk).astype(f32), axis=0, keepdims=True)
    masked = (coeffs_ref[...] * hit).T
    for ct, (first, n) in zip(cts, CHUNKS):
        ct[core, zy] = masked[first:first + n]

    pl.semaphore_wait(barrier, len(GATHER) + len(PEERS) + 1)

    sends, y_sends, z_sends = [], [None], [None]

    def across_y(k):
        copy = pltpu.make_async_remote_copy(
            src_ref=cts[k].at[core, zy], dst_ref=cts[k].at[core, zy],
            send_sem=y_send.at[k - 1], recv_sem=y_recv.at[k - 1],
            device_id=gather_peer(1, 0, 1), device_id_type=MESH,
        )
        copy.start()
        y_sends.append(copy)

    across_y(1)
    for i, (oy, dz) in enumerate(GATHER):
        copy = pltpu.make_async_remote_copy(
            src_ref=ct0.at[core, zy], dst_ref=ct0.at[core, zy],
            send_sem=g_send.at[i], recv_sem=g_recv.at[i],
            device_id=gather_peer(oy, dz, 1), device_id_type=MESH,
        )
        copy.start()
        sends.append(copy)
    across_y(2)

    def along_z(k):
        y_sends[k].wait_recv()
        both = cts[k].at[core, pl.ds(z * 2, 2)]
        z_sends.append([])
        for i, dz in enumerate((2, 1, 3)):
            copy = pltpu.make_async_remote_copy(
                src_ref=both, dst_ref=both,
                send_sem=z_send.at[k - 1, i], recv_sem=z_recv.at[k - 1, i],
                device_id=gather_peer(0, dz, 1), device_id_type=MESH,
            )
            copy.start()
            z_sends[k].append(copy)

    def split_ints(g):
        loads[g].wait()

        def part(t, carry):
            at = pl.multiple_of(g * 256 + t * 64, 64)
            for p in range(PAIRS):
                hi, lo = split(ints[pl.ds(at * PAIRS + p, 64, stride=PAIRS), :])
                i_hi[pl.ds(at, 64), p * S:(p + 1) * S] = hi
                i_lo[pl.ds(at, 64), p * S:(p + 1) * S] = lo
            return carry

        lax.fori_loop(0, 4, part, 0)

    def forward(k):
        for copy in sends if k == 0 else z_sends[k]:
            copy.wait_recv()
        copy = pltpu.make_async_remote_copy(
            src_ref=cts[k].at[core], dst_ref=cts[k].at[core],
            send_sem=c_send.at[k], recv_sem=c_recv.at[k],
            device_id=sibling, device_id_type=MESH,
        )
        copy.start()
        return copy

    def assemble(k, copy, *places):
        copy.wait_recv()
        ct, n = cts[k], CHUNKS[k][1]
        for p in range(PAIRS):
            b = pair_ref[0, p]
            parts = split(ct[lax.rem(b, 2), b // 2])
            for lhs, *firsts in places:
                for first, part in zip(firsts, parts):
                    lhs[first:first + n, p * S:(p + 1) * S] = part

    def send(k, source, target, at, count):
        for dx, dy in PEERS:
            a = aux_peer(dx, dy)
            pltpu.make_async_remote_copy(
                src_ref=source(a, pl.ds(at, count)), dst_ref=target(pl.ds(aux * SHARE + at, count)),
                send_sem=a_send.at[k], recv_sem=a_recv.at[k],
                device_id=(blk, a), device_id_type=MESH,
            ).start()
        pltpu.make_async_copy(
            source(aux, pl.ds(at, count)), target(pl.ds(aux * SHARE + at, count)), a_recv.at[k]
        ).start()

    def send01(first, rows):
        o = pl.ds(first, rows)
        return functools.partial(
            send, 0, lambda a, at: half01.at[a, at, o], lambda at: recv01.at[at, o]
        )

    def send23(i):
        return functools.partial(
            send, 1 + i, lambda a, at: half23.at[i, a, at], lambda at: recv23.at[i, at]
        )

    def products(lhs, q, low, high, step):
        n = lhs.shape[0] // 2
        quarters = [q + r for r in range(n // QROWS)]

        def group(g, carry):
            at = pl.ds(pl.multiple_of(g * step * S, step * S), step * S)
            both = jnp.zeros((2 * n, step * S), f32)
            cross = jnp.zeros((n, step * S), f32)
            for j in range(K // 256):
                c = slice(j * 256, (j + 1) * 256)
                both += lax.dot_general(lhs[:, c], i_hi[at, c], NT, preferred_element_type=f32)
                cross += lax.dot_general(lhs[0:n, c], i_lo[at, c], NT, preferred_element_type=f32)
            total = both[:n] + (both[n:] + cross)
            for j in range(step):
                for i, r in enumerate(quarters):
                    rows = total[i * QROWS:(i + 1) * QROWS, j * S:(j + 1) * S].reshape(8, 8, S)
                    if r < 2:
                        half01[:, g * step + j, r * 8:r * 8 + 8] = rows
                    else:
                        half23[r - 2, :, g * step + j] = rows
            if q < 2:
                send01(q * 8, 8 * len(quarters))(g * step, step)
            else:
                send23(0)(g * step, step)
            return carry

        lax.fori_loop(low // step, high // step, group, 0)

    inputs[2].wait()
    metric = split(metric_ref[...])

    def arrived(k, buffer):
        pltpu.make_async_copy(buffer, buffer, a_recv.at[k]).wait()

    def finish(buffer, first):
        n = buffer.shape[1]
        flat = buffer.reshape(NAUX * n, S)
        parts = [flat[pl.ds(first + t, NAUX, stride=n), :] for t in range(8)]
        fitted = dot3(metric, split(jnp.concatenate(parts, axis=1)))
        fitted = jnp.concatenate([fitted[:, t * S:(t + 1) * S] for t in range(8)], axis=0)
        turned = jnp.concatenate([v.T for v in parts], axis=1)
        return dot3(split(turned), split(fitted))

    for g in range(4):
        split_ints(g)
    along_z(1)
    split_ints(4)
    f0 = forward(0)
    for g in range(5, NGROUPS):
        split_ints(g)
    along_z(2)
    assemble(0, f0, (lhs0, 0, QROWS), (lhs01, 0, 2 * QROWS))
    products(lhs0, 0, 0, 4, 4)
    f1 = forward(1)
    products(lhs0, 0, 4, 8, 4)
    assemble(1, f1, (lhs1, 0, QROWS), (lhs01, QROWS, 3 * QROWS))
    products(lhs01, 0, 8, SHARE, 4)
    products(lhs1, 1, 0, 4, 4)
    f2 = forward(2)
    products(lhs1, 1, 4, 8, 4)
    assemble(2, f2, (lhs2, 0, 2 * QROWS))
    products(lhs2, 2, 0, 8, 4)
    send23(1)(0, 8)
    products(lhs2, 2, 8, SHARE, 4)
    send23(1)(8, 8)
    arrived(0, recv01)
    band[...] = finish(recv01, 0)
    band[...] += finish(recv01, 8)
    for i in range(2):
        arrived(1 + i, recv23.at[i])
        band[...] += finish(recv23.at[i], 0)

    last = []
    for i, (dx, dy) in enumerate(PEERS):
        a = aux_peer(dx, dy)
        copy = pltpu.make_async_remote_copy(
            src_ref=band.at[pl.ds(pl.multiple_of(a * 16, 16), 16)], dst_ref=bands.at[i],
            send_sem=b_send.at[i], recv_sem=b_recv.at[i],
            device_id=(blk, a), device_id_type=MESH,
        )
        copy.start()
        last.append(copy)
    total = band[pl.ds(pl.multiple_of(aux * 16, 16), 16), :]
    for i, copy in enumerate(last):
        copy.wait_recv()
        total += bands[i]
    out_ref[...] = total

    for copy in sends + y_sends[1:] + z_sends[1] + z_sends[2] + [f0, f1, f2] + last:
        copy.wait_send()
    for k, sent in enumerate((half01.at[pl.ds(0, 7)], half23.at[0, pl.ds(0, 7)], half23.at[1, pl.ds(0, 7)])):
        pltpu.make_async_copy(sent, sent, a_send.at[k]).wait()


def local(coeffs, integrals, metric, pair_blocks, support):
    vmem = pl.BlockSpec(memory_space=pltpu.VMEM)
    dma = pltpu.SemaphoreType.DMA
    return pl.pallas_call(
        kernel,
        name="exchange",
        out_shape=jax.ShapeDtypeStruct((16, S), f32),
        in_specs=[pl.BlockSpec(memory_space=pltpu.SMEM)] + [pl.BlockSpec(memory_space=pl.ANY)] * 4,
        out_specs=vmem,
        scratch_shapes=[
            pltpu.VMEM((S, NOCC), f32),
            pltpu.VMEM((4, NOCC), jnp.int32),
            pltpu.VMEM((S, S), f32),
            pltpu.VMEM((SHARE * S * PAIRS, S), f32),
            pltpu.VMEM((SHARE * S, K), bf16),
            pltpu.VMEM((SHARE * S, K), bf16),
            *[pltpu.VMEM((2, 8, n, S), f32) for _, n in CHUNKS],
            *[pltpu.VMEM((2 * n, K), bf16) for n in (64, 64, 128, 128)],
            pltpu.VMEM((8, SHARE, 16, S), f32),
            pltpu.VMEM((2, 8, SHARE, 8, S), f32),
            pltpu.VMEM((NAUX, 16, S), f32),
            pltpu.VMEM((2, NAUX, 8, S), f32),
            pltpu.VMEM((S, S), f32),
            pltpu.VMEM((len(PEERS), 16, S), f32),
            dma((3,)),
            dma((NGROUPS,)),
            dma((len(GATHER),)),
            dma((len(GATHER),)),
            dma((2,)),
            dma((2,)),
            dma((2, 3)),
            dma((2, 3)),
            dma((3,)),
            dma((3,)),
            dma((3,)),
            dma((3,)),
            dma((len(PEERS),)),
            dma((len(PEERS),)),
        ],
        compiler_params=pltpu.CompilerParams(
            collective_id=0, has_side_effects=True, vmem_limit_bytes=56 * 2**20
        ),
    )(pair_blocks, coeffs, support.T, metric, integrals.reshape(SHARE * S * PAIRS, S))


def solution(mesh):
    return jax.shard_map(
        local,
        mesh=mesh,
        in_specs=(P("blk", None), P("blk", "aux", None, None, None), P(), P("blk", None), P()),
        out_specs=P(("blk", "aux"), None),
        check_vma=False,
    )
```

```python
import functools

import jax
import jax.numpy as jnp
from jax import lax
from jax.experimental import pallas as pl
from jax.experimental.pallas import tpu as pltpu
from jax.sharding import PartitionSpec as P

S = 128
PAIRS = 16
NOCC = 256
SHARE = 16
NAUX = 128
K = PAIRS * S
QROWS = 64
CHUNKS = ((0, 64), (64, 64), (128, 128))
NGROUPS = 8
f32, bf16 = jnp.float32, jnp.bfloat16
MESH = pl.DeviceIdType.MESH
NN = (((1,), (0,)), ((), ()))
NT = (((1,), (1,)), ((), ()))
PEERS = [(dx, dy) for dy in (1, 0) for dx in (2, 1, 3, 0) if (dx, dy) != (0, 0)]
GATHER = [(1, 2), (1, 1), (1, 3), (0, 2), (0, 1), (0, 3), (1, 0)]


def split(v):
    hi = v.astype(bf16)
    return hi, (v - hi.astype(f32)).astype(bf16)


def dot3(a, b, dims=NN):
    ah, al = a
    bh, bl = b
    d = functools.partial(lax.dot_general, dimension_numbers=dims, preferred_element_type=f32)
    return d(ah, bh) + (d(ah, bl) + d(al, bh))


def kernel(
    pair_ref, coeffs_hbm, support_hbm, metric_hbm, ints_ref, out_ref,
    coeffs_ref, support_ref, metric_ref, ints, i_hi, i_lo, ct0, ct1, ct2, lhs0, lhs1, lhs01, lhs2, half01, half23, recv01, recv23, band, bands,
    in_sem, i_sem, g_send, g_recv, y_send, y_recv, z_send, z_recv, c_send, c_recv, a_send, a_recv, b_send, b_recv,
):
    blk, aux = lax.axis_index("blk"), lax.axis_index("aux")
    core, ylo, z = lax.rem(blk, 2), lax.rem(blk // 2, 2), blk // 4
    x, yhi = lax.rem(aux, 4), aux // 4
    y = yhi * 2 + ylo
    zy = z * 2 + ylo
    cts = (ct0, ct1, ct2)

    def device(x, y, z, core):
        return ((z * 2 + lax.rem(y, 2)) * 2 + core, (y // 2) * 4 + x)

    def aux_peer(dx, dy):
        return lax.rem(yhi + dy, 2) * 4 + lax.rem(x + dx, 4)

    def gather_peer(oy, dz, sign):
        step = oy * (1 + 2 * core) if sign > 0 else oy * (3 - 2 * core)
        return device(x, lax.rem(y + step, 4), lax.rem(z + (dz if sign > 0 else 4 - dz), 4), core)

    sibling = (blk + 1 - 2 * core, aux)

    inputs = []
    for i, (src, dst) in enumerate(
        ((coeffs_hbm, coeffs_ref), (support_hbm, support_ref), (metric_hbm, metric_ref))
    ):
        load = pltpu.make_async_copy(src, dst, in_sem.at[i])
        load.start()
        inputs.append(load)
    barrier = pltpu.get_barrier_semaphore()
    for oy, dz in GATHER:
        pl.semaphore_signal(barrier, inc=1, device_id=gather_peer(oy, dz, -1), device_id_type=MESH)
    for dx, dy in PEERS:
        pl.semaphore_signal(barrier, inc=1, device_id=(blk, aux_peer(dx, dy)), device_id_type=MESH)
    pl.semaphore_signal(barrier, inc=1, device_id=sibling, device_id_type=MESH)

    inputs[0].wait()
    inputs[1].wait()
    loads = []
    rows = SHARE * S * PAIRS // NGROUPS
    for g in range(NGROUPS):
        load = pltpu.make_async_copy(
            ints_ref.at[pl.ds(g * rows, rows)], ints.at[pl.ds(g * rows, rows)], i_sem.at[g]
        )
        load.start()
        loads.append(load)

    hit = jnp.max((support_ref[...] == blk).astype(f32), axis=0, keepdims=True)
    masked = (coeffs_ref[...] * hit).T
    for ct, (first, n) in zip(cts, CHUNKS):
        ct[core, zy] = masked[first:first + n]

    pl.semaphore_wait(barrier, len(GATHER) + len(PEERS) + 1)

    sends, y_sends, z_sends = [], [None], [None]

    def across_y(k):
        copy = pltpu.make_async_remote_copy(
            src_ref=cts[k].at[core, zy], dst_ref=cts[k].at[core, zy],
            send_sem=y_send.at[k - 1], recv_sem=y_recv.at[k - 1],
            device_id=gather_peer(1, 0, 1), device_id_type=MESH,
        )
        copy.start()
        y_sends.append(copy)

    across_y(1)
    for i, (oy, dz) in enumerate(GATHER):
        copy = pltpu.make_async_remote_copy(
            src_ref=ct0.at[core, zy], dst_ref=ct0.at[core, zy],
            send_sem=g_send.at[i], recv_sem=g_recv.at[i],
            device_id=gather_peer(oy, dz, 1), device_id_type=MESH,
        )
        copy.start()
        sends.append(copy)
    across_y(2)

    def along_z(k):
        y_sends[k].wait_recv()
        both = cts[k].at[core, pl.ds(z * 2, 2)]
        z_sends.append([])
        for i, dz in enumerate((2, 1, 3)):
            copy = pltpu.make_async_remote_copy(
                src_ref=both, dst_ref=both,
                send_sem=z_send.at[k - 1, i], recv_sem=z_recv.at[k - 1, i],
                device_id=gather_peer(0, dz, 1), device_id_type=MESH,
            )
            copy.start()
            z_sends[k].append(copy)

    def split_ints(g):
        loads[g].wait()

        def part(t, carry):
            at = pl.multiple_of(g * 256 + t * 64, 64)
            for p in range(PAIRS):
                hi, lo = split(ints[pl.ds(at * PAIRS + p, 64, stride=PAIRS), :])
                i_hi[pl.ds(at, 64), p * S:(p + 1) * S] = hi
                i_lo[pl.ds(at, 64), p * S:(p + 1) * S] = lo
            return carry

        lax.fori_loop(0, 4, part, 0)

    def forward(k):
        for copy in sends if k == 0 else z_sends[k]:
            copy.wait_recv()
        copy = pltpu.make_async_remote_copy(
            src_ref=cts[k].at[core], dst_ref=cts[k].at[core],
            send_sem=c_send.at[k], recv_sem=c_recv.at[k],
            device_id=sibling, device_id_type=MESH,
        )
        copy.start()
        return copy

    def assemble(k, copy, *places):
        copy.wait_recv()
        ct, n = cts[k], CHUNKS[k][1]
        for p in range(PAIRS):
            b = pair_ref[0, p]
            parts = split(ct[lax.rem(b, 2), b // 2])
            for lhs, *firsts in places:
                for first, part in zip(firsts, parts):
                    lhs[first:first + n, p * S:(p + 1) * S] = part

    def send(k, source, target, at, count):
        for dx, dy in PEERS:
            a = aux_peer(dx, dy)
            pltpu.make_async_remote_copy(
                src_ref=source(a, pl.ds(at, count)), dst_ref=target(pl.ds(aux * SHARE + at, count)),
                send_sem=a_send.at[k], recv_sem=a_recv.at[k],
                device_id=(blk, a), device_id_type=MESH,
            ).start()
        pltpu.make_async_copy(
            source(aux, pl.ds(at, count)), target(pl.ds(aux * SHARE + at, count)), a_recv.at[k]
        ).start()

    def send01(first, rows):
        o = pl.ds(first, rows)
        return functools.partial(
            send, 0, lambda a, at: half01.at[a, at, o], lambda at: recv01.at[at, o]
        )

    def send23(i):
        return functools.partial(
            send, 1 + i, lambda a, at: half23.at[i, a, at], lambda at: recv23.at[i, at]
        )

    def products(lhs, q, low, high, step):
        n = lhs.shape[0] // 2
        quarters = [q + r for r in range(n // QROWS)]

        def group(g, carry):
            at = pl.ds(pl.multiple_of(g * step * S, step * S), step * S)
            both = jnp.zeros((2 * n, step * S), f32)
            cross = jnp.zeros((n, step * S), f32)
            for j in range(K // 256):
                c = slice(j * 256, (j + 1) * 256)
                both += lax.dot_general(lhs[:, c], i_hi[at, c], NT, preferred_element_type=f32)
                cross += lax.dot_general(lhs[0:n, c], i_lo[at, c], NT, preferred_element_type=f32)
            total = both[:n] + (both[n:] + cross)
            for j in range(step):
                for i, r in enumerate(quarters):
                    rows = total[i * QROWS:(i + 1) * QROWS, j * S:(j + 1) * S].reshape(8, 8, S)
                    if r < 2:
                        half01[:, g * step + j, r * 8:r * 8 + 8] = rows
                    else:
                        half23[r - 2, :, g * step + j] = rows
            if q < 2:
                send01(q * 8, 8 * len(quarters))(g * step, step)
            else:
                send23(0)(g * step, step)
            return carry

        lax.fori_loop(low // step, high // step, group, 0)

    inputs[2].wait()
    metric = split(metric_ref[...])

    def arrived(k, buffer):
        pltpu.make_async_copy(buffer, buffer, a_recv.at[k]).wait()

    def finish(buffer, first):
        n = buffer.shape[1]
        flat = buffer.reshape(NAUX * n, S)
        parts = [flat[pl.ds(first + t, NAUX, stride=n), :] for t in range(8)]
        fitted = dot3(metric, split(jnp.concatenate(parts, axis=1)))
        fitted = jnp.concatenate([fitted[:, t * S:(t + 1) * S] for t in range(8)], axis=0)
        turned = jnp.concatenate([v.T for v in parts], axis=1)
        return dot3(split(turned), split(fitted))

    for g in range(4):
        split_ints(g)
    along_z(1)
    split_ints(4)
    f0 = forward(0)
    split_ints(5)
    along_z(2)
    assemble(0, f0, (lhs0, 0, QROWS), (lhs01, 0, 2 * QROWS))
    products(lhs0, 0, 0, 4, 4)
    f1 = forward(1)
    split_ints(6)
    split_ints(7)
    products(lhs0, 0, 4, 8, 4)
    assemble(1, f1, (lhs1, 0, QROWS), (lhs01, QROWS, 3 * QROWS))
    products(lhs01, 0, 8, SHARE, 4)
    products(lhs1, 1, 0, 4, 4)
    f2 = forward(2)
    products(lhs1, 1, 4, 8, 4)
    assemble(2, f2, (lhs2, 0, 2 * QROWS))
    products(lhs2, 2, 0, 8, 4)
    send23(1)(0, 8)
    products(lhs2, 2, 8, SHARE, 4)
    send23(1)(8, 8)
    arrived(0, recv01)
    band[...] = finish(recv01, 0)
    band[...] += finish(recv01, 8)
    for i in range(2):
        arrived(1 + i, recv23.at[i])
        band[...] += finish(recv23.at[i], 0)

    last = []
    for i, (dx, dy) in enumerate(PEERS):
        a = aux_peer(dx, dy)
        copy = pltpu.make_async_remote_copy(
            src_ref=band.at[pl.ds(pl.multiple_of(a * 16, 16), 16)], dst_ref=bands.at[i],
            send_sem=b_send.at[i], recv_sem=b_recv.at[i],
            device_id=(blk, a), device_id_type=MESH,
        )
        copy.start()
        last.append(copy)
    total = band[pl.ds(pl.multiple_of(aux * 16, 16), 16), :]
    for i, copy in enumerate(last):
        copy.wait_recv()
        total += bands[i]
    out_ref[...] = total

    for copy in sends + y_sends[1:] + z_sends[1] + z_sends[2] + [f0, f1, f2] + last:
        copy.wait_send()
    for k, sent in enumerate((half01.at[pl.ds(0, 7)], half23.at[0, pl.ds(0, 7)], half23.at[1, pl.ds(0, 7)])):
        pltpu.make_async_copy(sent, sent, a_send.at[k]).wait()


def local(coeffs, integrals, metric, pair_blocks, support):
    vmem = pl.BlockSpec(memory_space=pltpu.VMEM)
    dma = pltpu.SemaphoreType.DMA
    return pl.pallas_call(
        kernel,
        name="exchange",
        out_shape=jax.ShapeDtypeStruct((16, S), f32),
        in_specs=[pl.BlockSpec(memory_space=pltpu.SMEM)] + [pl.BlockSpec(memory_space=pl.ANY)] * 4,
        out_specs=vmem,
        scratch_shapes=[
            pltpu.VMEM((S, NOCC), f32),
            pltpu.VMEM((4, NOCC), jnp.int32),
            pltpu.VMEM((S, S), f32),
            pltpu.VMEM((SHARE * S * PAIRS, S), f32),
            pltpu.VMEM((SHARE * S, K), bf16),
            pltpu.VMEM((SHARE * S, K), bf16),
            *[pltpu.VMEM((2, 8, n, S), f32) for _, n in CHUNKS],
            *[pltpu.VMEM((2 * n, K), bf16) for n in (64, 64, 128, 128)],
            pltpu.VMEM((8, SHARE, 16, S), f32),
            pltpu.VMEM((2, 8, SHARE, 8, S), f32),
            pltpu.VMEM((NAUX, 16, S), f32),
            pltpu.VMEM((2, NAUX, 8, S), f32),
            pltpu.VMEM((S, S), f32),
            pltpu.VMEM((len(PEERS), 16, S), f32),
            dma((3,)),
            dma((NGROUPS,)),
            dma((len(GATHER),)),
            dma((len(GATHER),)),
            dma((2,)),
            dma((2,)),
            dma((2, 3)),
            dma((2, 3)),
            dma((3,)),
            dma((3,)),
            dma((3,)),
            dma((3,)),
            dma((len(PEERS),)),
            dma((len(PEERS),)),
        ],
        compiler_params=pltpu.CompilerParams(
            collective_id=0, has_side_effects=True, vmem_limit_bytes=56 * 2**20
        ),
    )(pair_blocks, coeffs, support.T, metric, integrals.reshape(SHARE * S * PAIRS, S))


def solution(mesh):
    return jax.shard_map(
        local,
        mesh=mesh,
        in_specs=(P("blk", None), P("blk", "aux", None, None, None), P(), P("blk", None), P()),
        out_specs=P(("blk", "aux"), None),
        check_vma=False,
    )
```

```python
import functools

import jax
import jax.numpy as jnp
from jax import lax
from jax.experimental import pallas as pl
from jax.experimental.pallas import tpu as pltpu
from jax.sharding import PartitionSpec as P

S = 128
PAIRS = 16
NOCC = 256
SHARE = 16
NAUX = 128
K = PAIRS * S
QROWS = 64
CHUNKS = ((0, 64), (64, 64), (128, 128))
NGROUPS = 8
f32, bf16 = jnp.float32, jnp.bfloat16
MESH = pl.DeviceIdType.MESH
NN = (((1,), (0,)), ((), ()))
NT = (((1,), (1,)), ((), ()))
PEERS = [(dx, dy) for dy in (1, 0) for dx in (2, 1, 3, 0) if (dx, dy) != (0, 0)]
GATHER = [(1, 2), (1, 1), (1, 3), (0, 2), (0, 1), (0, 3), (1, 0)]


def split(v):
    hi = v.astype(bf16)
    return hi, (v - hi.astype(f32)).astype(bf16)


def dot3(a, b, dims=NN):
    ah, al = a
    bh, bl = b
    d = functools.partial(lax.dot_general, dimension_numbers=dims, preferred_element_type=f32)
    return d(ah, bh) + (d(ah, bl) + d(al, bh))


def kernel(
    pair_ref, coeffs_hbm, support_hbm, metric_hbm, ints_ref, out_ref,
    coeffs_ref, support_ref, metric_ref, ints, i_hi, i_lo, ct0, ct1, ct2, lhs0, lhs1, lhs01, lhs2, half01, half23, recv01, recv23, band, bands,
    in_sem, i_sem, g_send, g_recv, y_send, y_recv, z_send, z_recv, c_send, c_recv, a_send, a_recv, b_send, b_recv,
):
    blk, aux = lax.axis_index("blk"), lax.axis_index("aux")
    core, ylo, z = lax.rem(blk, 2), lax.rem(blk // 2, 2), blk // 4
    x, yhi = lax.rem(aux, 4), aux // 4
    y = yhi * 2 + ylo
    zy = z * 2 + ylo
    cts = (ct0, ct1, ct2)

    def device(x, y, z, core):
        return ((z * 2 + lax.rem(y, 2)) * 2 + core, (y // 2) * 4 + x)

    def aux_peer(dx, dy):
        return lax.rem(yhi + dy, 2) * 4 + lax.rem(x + dx, 4)

    def gather_peer(oy, dz, sign):
        step = oy * (1 + 2 * core) if sign > 0 else oy * (3 - 2 * core)
        return device(x, lax.rem(y + step, 4), lax.rem(z + (dz if sign > 0 else 4 - dz), 4), core)

    sibling = (blk + 1 - 2 * core, aux)

    barrier = pltpu.get_barrier_semaphore()
    for oy, dz in GATHER:
        pl.semaphore_signal(barrier, inc=1, device_id=gather_peer(oy, dz, -1), device_id_type=MESH)
    for dx, dy in PEERS:
        pl.semaphore_signal(barrier, inc=1, device_id=(blk, aux_peer(dx, dy)), device_id_type=MESH)
    pl.semaphore_signal(barrier, inc=1, device_id=sibling, device_id_type=MESH)

    inputs = []
    for i, (src, dst) in enumerate(
        ((coeffs_hbm, coeffs_ref), (support_hbm, support_ref), (metric_hbm, metric_ref))
    ):
        load = pltpu.make_async_copy(src, dst, in_sem.at[i])
        load.start()
        inputs.append(load)
    inputs[0].wait()
    inputs[1].wait()
    loads = []
    rows = SHARE * S * PAIRS // NGROUPS
    for g in range(NGROUPS):
        load = pltpu.make_async_copy(
            ints_ref.at[pl.ds(g * rows, rows)], ints.at[pl.ds(g * rows, rows)], i_sem.at[g]
        )
        load.start()
        loads.append(load)

    hit = jnp.max((support_ref[...] == blk).astype(f32), axis=0, keepdims=True)
    masked = (coeffs_ref[...] * hit).T
    for ct, (first, n) in zip(cts, CHUNKS):
        ct[core, zy] = masked[first:first + n]

    pl.semaphore_wait(barrier, len(GATHER) + len(PEERS) + 1)

    sends, y_sends, z_sends = [], [None], [None]

    def across_y(k):
        copy = pltpu.make_async_remote_copy(
            src_ref=cts[k].at[core, zy], dst_ref=cts[k].at[core, zy],
            send_sem=y_send.at[k - 1], recv_sem=y_recv.at[k - 1],
            device_id=gather_peer(1, 0, 1), device_id_type=MESH,
        )
        copy.start()
        y_sends.append(copy)

    across_y(1)
    for i, (oy, dz) in enumerate(GATHER):
        copy = pltpu.make_async_remote_copy(
            src_ref=ct0.at[core, zy], dst_ref=ct0.at[core, zy],
            send_sem=g_send.at[i], recv_sem=g_recv.at[i],
            device_id=gather_peer(oy, dz, 1), device_id_type=MESH,
        )
        copy.start()
        sends.append(copy)
    across_y(2)

    def along_z(k):
        y_sends[k].wait_recv()
        both = cts[k].at[core, pl.ds(z * 2, 2)]
        z_sends.append([])
        for i, dz in enumerate((2, 1, 3)):
            copy = pltpu.make_async_remote_copy(
                src_ref=both, dst_ref=both,
                send_sem=z_send.at[k - 1, i], recv_sem=z_recv.at[k - 1, i],
                device_id=gather_peer(0, dz, 1), device_id_type=MESH,
            )
            copy.start()
            z_sends[k].append(copy)

    def split_ints(g):
        loads[g].wait()

        def part(t, carry):
            at = pl.multiple_of(g * 256 + t * 64, 64)
            for p in range(PAIRS):
                hi, lo = split(ints[pl.ds(at * PAIRS + p, 64, stride=PAIRS), :])
                i_hi[pl.ds(at, 64), p * S:(p + 1) * S] = hi
                i_lo[pl.ds(at, 64), p * S:(p + 1) * S] = lo
            return carry

        lax.fori_loop(0, 4, part, 0)

    def forward(k):
        for copy in sends if k == 0 else z_sends[k]:
            copy.wait_recv()
        copy = pltpu.make_async_remote_copy(
            src_ref=cts[k].at[core], dst_ref=cts[k].at[core],
            send_sem=c_send.at[k], recv_sem=c_recv.at[k],
            device_id=sibling, device_id_type=MESH,
        )
        copy.start()
        return copy

    def assemble(k, copy, *places):
        copy.wait_recv()
        ct, n = cts[k], CHUNKS[k][1]
        for p in range(PAIRS):
            b = pair_ref[0, p]
            parts = split(ct[lax.rem(b, 2), b // 2])
            for lhs, *firsts in places:
                for first, part in zip(firsts, parts):
                    lhs[first:first + n, p * S:(p + 1) * S] = part

    def send(k, source, target, at, count):
        for dx, dy in PEERS:
            a = aux_peer(dx, dy)
            pltpu.make_async_remote_copy(
                src_ref=source(a, pl.ds(at, count)), dst_ref=target(pl.ds(aux * SHARE + at, count)),
                send_sem=a_send.at[k], recv_sem=a_recv.at[k],
                device_id=(blk, a), device_id_type=MESH,
            ).start()
        pltpu.make_async_copy(
            source(aux, pl.ds(at, count)), target(pl.ds(aux * SHARE + at, count)), a_recv.at[k]
        ).start()

    def send01(first, rows):
        o = pl.ds(first, rows)
        return functools.partial(
            send, 0, lambda a, at: half01.at[a, at, o], lambda at: recv01.at[at, o]
        )

    def send23(i):
        return functools.partial(
            send, 1 + i, lambda a, at: half23.at[i, a, at], lambda at: recv23.at[i, at]
        )

    def products(lhs, q, low, high, step):
        n = lhs.shape[0] // 2
        quarters = [q + r for r in range(n // QROWS)]

        def group(g, carry):
            at = pl.ds(pl.multiple_of(g * step * S, step * S), step * S)
            both = jnp.zeros((2 * n, step * S), f32)
            cross = jnp.zeros((n, step * S), f32)
            for j in range(K // 256):
                c = slice(j * 256, (j + 1) * 256)
                both += lax.dot_general(lhs[:, c], i_hi[at, c], NT, preferred_element_type=f32)
                cross += lax.dot_general(lhs[0:n, c], i_lo[at, c], NT, preferred_element_type=f32)
            total = both[:n] + (both[n:] + cross)
            for j in range(step):
                for i, r in enumerate(quarters):
                    rows = total[i * QROWS:(i + 1) * QROWS, j * S:(j + 1) * S].reshape(8, 8, S)
                    if r < 2:
                        half01[:, g * step + j, r * 8:r * 8 + 8] = rows
                    else:
                        half23[r - 2, :, g * step + j] = rows
            if q < 2:
                send01(q * 8, 8 * len(quarters))(g * step, step)
            else:
                send23(0)(g * step, step)
            return carry

        lax.fori_loop(low // step, high // step, group, 0)

    inputs[2].wait()
    metric = split(metric_ref[...])

    def arrived(k, buffer):
        pltpu.make_async_copy(buffer, buffer, a_recv.at[k]).wait()

    def finish(buffer, first):
        n = buffer.shape[1]
        flat = buffer.reshape(NAUX * n, S)
        parts = [flat[pl.ds(first + t, NAUX, stride=n), :] for t in range(8)]
        fitted = dot3(metric, split(jnp.concatenate(parts, axis=1)))
        fitted = jnp.concatenate([fitted[:, t * S:(t + 1) * S] for t in range(8)], axis=0)
        turned = jnp.concatenate([v.T for v in parts], axis=1)
        return dot3(split(turned), split(fitted))

    for g in range(4):
        split_ints(g)
    along_z(1)
    split_ints(4)
    f0 = forward(0)
    for g in range(5, NGROUPS):
        split_ints(g)
    along_z(2)
    assemble(0, f0, (lhs0, 0, QROWS), (lhs01, 0, 2 * QROWS))
    products(lhs0, 0, 0, 4, 4)
    f1 = forward(1)
    products(lhs0, 0, 4, 8, 4)
    assemble(1, f1, (lhs1, 0, QROWS), (lhs01, QROWS, 3 * QROWS))
    products(lhs01, 0, 8, SHARE, 4)
    products(lhs1, 1, 0, 4, 4)
    f2 = forward(2)
    products(lhs1, 1, 4, 8, 4)
    assemble(2, f2, (lhs2, 0, 2 * QROWS))
    products(lhs2, 2, 0, 8, 4)
    send23(1)(0, 8)
    products(lhs2, 2, 8, SHARE, 4)
    send23(1)(8, 8)
    arrived(0, recv01)
    band[...] = finish(recv01, 0)
    band[...] += finish(recv01, 8)
    for i in range(2):
        arrived(1 + i, recv23.at[i])
        band[...] += finish(recv23.at[i], 0)

    last = []
    for i, (dx, dy) in enumerate(PEERS):
        a = aux_peer(dx, dy)
        copy = pltpu.make_async_remote_copy(
            src_ref=band.at[pl.ds(pl.multiple_of(a * 16, 16), 16)], dst_ref=bands.at[i],
            send_sem=b_send.at[i], recv_sem=b_recv.at[i],
            device_id=(blk, a), device_id_type=MESH,
        )
        copy.start()
        last.append(copy)
    total = band[pl.ds(pl.multiple_of(aux * 16, 16), 16), :]
    for i, copy in enumerate(last):
        copy.wait_recv()
        total += bands[i]
    out_ref[...] = total

    for copy in sends + y_sends[1:] + z_sends[1] + z_sends[2] + [f0, f1, f2] + last:
        copy.wait_send()
    for k, sent in enumerate((half01.at[pl.ds(0, 7)], half23.at[0, pl.ds(0, 7)], half23.at[1, pl.ds(0, 7)])):
        pltpu.make_async_copy(sent, sent, a_send.at[k]).wait()


def local(coeffs, integrals, metric, pair_blocks, support):
    vmem = pl.BlockSpec(memory_space=pltpu.VMEM)
    dma = pltpu.SemaphoreType.DMA
    return pl.pallas_call(
        kernel,
        name="exchange",
        out_shape=jax.ShapeDtypeStruct((16, S), f32),
        in_specs=[pl.BlockSpec(memory_space=pltpu.SMEM)] + [pl.BlockSpec(memory_space=pl.ANY)] * 4,
        out_specs=vmem,
        scratch_shapes=[
            pltpu.VMEM((S, NOCC), f32),
            pltpu.VMEM((4, NOCC), jnp.int32),
            pltpu.VMEM((S, S), f32),
            pltpu.VMEM((SHARE * S * PAIRS, S), f32),
            pltpu.VMEM((SHARE * S, K), bf16),
            pltpu.VMEM((SHARE * S, K), bf16),
            *[pltpu.VMEM((2, 8, n, S), f32) for _, n in CHUNKS],
            *[pltpu.VMEM((2 * n, K), bf16) for n in (64, 64, 128, 128)],
            pltpu.VMEM((8, SHARE, 16, S), f32),
            pltpu.VMEM((2, 8, SHARE, 8, S), f32),
            pltpu.VMEM((NAUX, 16, S), f32),
            pltpu.VMEM((2, NAUX, 8, S), f32),
            pltpu.VMEM((S, S), f32),
            pltpu.VMEM((len(PEERS), 16, S), f32),
            dma((3,)),
            dma((NGROUPS,)),
            dma((len(GATHER),)),
            dma((len(GATHER),)),
            dma((2,)),
            dma((2,)),
            dma((2, 3)),
            dma((2, 3)),
            dma((3,)),
            dma((3,)),
            dma((3,)),
            dma((3,)),
            dma((len(PEERS),)),
            dma((len(PEERS),)),
        ],
        compiler_params=pltpu.CompilerParams(
            collective_id=0, has_side_effects=True, vmem_limit_bytes=56 * 2**20
        ),
    )(pair_blocks, coeffs, support.T, metric, integrals.reshape(SHARE * S * PAIRS, S))


def solution(mesh):
    return jax.shard_map(
        local,
        mesh=mesh,
        in_specs=(P("blk", None), P("blk", "aux", None, None, None), P(), P("blk", None), P()),
        out_specs=P(("blk", "aux"), None),
        check_vma=False,
    )
```
